32 devices in a mesh: groups: 2 (over y), wide: 8 (over z, x), narrow: 2 (over core).
Axes of the slice: x: 2, y: 2, z: 4, core: 2. Of those that a mesh axis runs over, the one named last changes fastest.
Arguments:
- tokens: bfloat16 [4096, 8192], P(('groups', 'wide'), 'narrow'), parts along dimension 0, may hold values from -6 to 6
- output_gradient: bfloat16 [4096, 1024], P(('groups', 'wide'), 'narrow'), parts along dimension 0, may hold values from -0.59765625 to 0.59765625
- value_weight: bfloat16 [8192, 1024], P('narrow', 'wide'), may hold values from -0.0625 to 0.0625
- adapter_down: bfloat16 [32, 8192, 64], P(('groups', 'wide'), 'narrow'), parts along dimension 0, may hold values from -0.0625 to 0.0625
- adapter_up: bfloat16 [32, 64, 1024], P(('groups', 'wide'), None, 'narrow'), parts along dimension 0, may hold values from -0.1875 to 0.1875
- counts: int32 [16, 16], P(('groups', 'wide')), parts along dimension 0, may hold values from 0 to 32, as said below
- holder_table: int32 [32], P('groups'), parts along dimension 0, may hold values from 0 to 15, each once
Outputs:
- mixed: bfloat16 [4096, 1024], P(('groups', 'wide'), 'narrow'), parts along dimension 0
- down_gradient: bfloat16 [32, 8192, 64], P(('groups', 'wide'), 'narrow'), parts along dimension 0
- up_gradient: bfloat16 [32, 64, 1024], P(('groups', 'wide'), None, 'narrow'), parts along dimension 0
The draws below stay inside these ranges and needn't reach their ends.
There are 2 independent parts, one for each index of `groups`. The reference program is written for one: setup_inputs(seed, part) draws one part's arguments, and reference() takes and returns one part's arrays. A program takes and returns all parts, laid end to end along the dimension named above; an argument that names none is the same for every part. Nothing has to cross between parts.
Inputs may be any that keep to these rules, and one draw needn't show every extreme that they name: counts[w, a] tokens of device w belong to adapter a and stand together in adapter order; each row sums to 256, and every row has an entry equal to 32. Adapter a's factors are row holder_table[a] of adapter_down and adapter_up, which lives on wide index holder_table[a] // 2.
All inputs are finite; a program needn't handle non-finite values.
Results may differ from the reference program's by a relative error of at most 0.005.
Values may be sent and summed in bfloat16 or wider, within the bound.
A program may use at most 64 MiB of HBM per device.

```python
import jax
import jax.numpy as jnp
from jax import lax

MODEL_WIDTH = 8192
VALUE_WIDTH = 1024
ADAPTER_RANK = 64
TOK_DEV = 256
ADAPTER_TOTAL = 16
CAP = 32
TOKEN_TOTAL = 2048
N_WIDE = 8


def draw_counts(key, part):
    key = jax.random.fold_in(key, 11)
    hot_key, noise_key, pick_key = jax.random.split(key, 3)
    hotness = jax.random.randint(hot_key, (ADAPTER_TOTAL,), 0, 4)
    noise = jax.random.randint(noise_key, (N_WIDE, ADAPTER_TOTAL, CAP), 0, 1024)
    forced = jax.random.randint(pick_key, (N_WIDE,), 0, ADAPTER_TOTAL)
    adapter_index = jnp.arange(ADAPTER_TOTAL, dtype=jnp.int32)
    boost = jnp.where(adapter_index[None, :] == forced[:, None], 4096, 0)
    units = ADAPTER_TOTAL * CAP
    score = (noise + 256 * hotness[None, :, None] + boost[:, :, None]) * units
    score = score + jnp.arange(units, dtype=jnp.int32).reshape(1, ADAPTER_TOTAL, CAP)
    flat = score.reshape(N_WIDE, units).astype(jnp.int32)
    top_values = lax.top_k(flat, TOK_DEV)[0]
    chosen = (flat >= top_values[:, -1:]).astype(jnp.int32)
    return chosen.reshape(N_WIDE, ADAPTER_TOTAL, CAP).sum(axis=2).astype(jnp.int32)


def block_scale(own_key, dims, pieces, smallest, high):
    def one(axis_at, shards_of):
        draws = jax.random.uniform(jax.random.fold_in(jax.random.fold_in(own_key, 6), axis_at), (shards_of,), jnp.float32, smallest / len(pieces), high / len(pieces))
        return jnp.repeat(jnp.exp(draws), dims[axis_at] // shards_of).reshape((-1,) + (1,) * (len(dims) - axis_at - 1))

    loudness = one(*pieces[0])
    for cut in pieces[1:]:
        loudness = loudness * one(*cut)
    return loudness


def centred(own_key, extent, scale, reach, shards=(), held_as=jnp.bfloat16):
    loudness = block_scale(own_key, extent, shards, -0.22, 0.18) if shards else 1.0
    drawn = jax.random.normal(own_key, extent, jnp.float32) * scale * loudness
    return jnp.minimum(jnp.maximum(drawn, -reach), reach).astype(held_as)


def setup_inputs(seed: int = 0, part: int = 0) -> dict:
    arg_keys = jax.random.split(jax.random.key(seed), 8)
    part_splits = jax.random.split(jax.random.fold_in(arg_keys[7], part), 8)
    tokens = centred(part_splits[0], (TOKEN_TOTAL, MODEL_WIDTH), 1.0, 6.0, ((0, 8), (1, 2)))
    output_gradient = centred(part_splits[1], (TOKEN_TOTAL, VALUE_WIDTH), 0.1, 0.59765625, ((0, 8), (1, 2)))
    value_weight = centred(arg_keys[2], (MODEL_WIDTH, VALUE_WIDTH), MODEL_WIDTH ** -0.5, 0.0625, ((0, 2), (1, 8)))
    adapter_down = centred(part_splits[3], (ADAPTER_TOTAL, MODEL_WIDTH, ADAPTER_RANK), MODEL_WIDTH ** -0.5, 0.0625, ((0, 8), (1, 2)))
    adapter_up = centred(part_splits[4], (ADAPTER_TOTAL, ADAPTER_RANK, VALUE_WIDTH), VALUE_WIDTH ** -0.5, 0.1875, ((0, 8), (2, 2)))
    counts = draw_counts(jax.random.fold_in(jax.random.fold_in(arg_keys[7], part), 71), part)
    holder_table = jax.random.permutation(part_splits[6], ADAPTER_TOTAL).astype(jnp.int32)
    return {"tokens": tokens, "output_gradient": output_gradient, "value_weight": value_weight, "adapter_down": adapter_down, "adapter_up": adapter_up, "counts": counts, "holder_table": holder_table}


adapter_scale = 2.0


def reference(tokens, output_gradient, value_weight, adapter_down, adapter_up, counts, holder_table):
    group_ends = jnp.cumsum(counts, axis=1).astype(jnp.int32)
    group_starts = (group_ends - counts).astype(jnp.int32)
    adapter_index = jnp.arange(ADAPTER_TOTAL, dtype=jnp.int32)
    inverse = jnp.zeros((ADAPTER_TOTAL,), jnp.int32).at[holder_table].set(adapter_index)
    offsets = jnp.arange(CAP, dtype=jnp.int32)
    device_base = (jnp.arange(N_WIDE, dtype=jnp.int32) * TOK_DEV)[:, None]

    def slot_grouped(holder_slot):
        adapter = inverse[holder_slot]
        starts = group_starts[:, adapter]
        sizes = counts[:, adapter]
        valid = offsets[None, :] < sizes[:, None]
        token_matrix = jnp.where(valid, device_base + starts[:, None] + offsets[None, :], TOKEN_TOTAL).reshape(-1).astype(jnp.int32)
        safe_rows = jnp.minimum(token_matrix, TOKEN_TOTAL - 1)
        keep = (token_matrix < TOKEN_TOTAL)[:, None]
        token_vectors = jnp.where(keep, tokens[safe_rows], jnp.zeros((), tokens.dtype))
        gradient_rows = jnp.where(keep, output_gradient[safe_rows], jnp.zeros((), output_gradient.dtype))
        down_factor = adapter_down[holder_slot]
        up_factor = adapter_up[holder_slot]
        rank_inputs = jnp.dot(token_vectors, down_factor, preferred_element_type=jnp.float32)
        rank_outputs = jnp.dot(gradient_rows, up_factor.T, preferred_element_type=jnp.float32)
        adapter_piece = adapter_scale * jnp.dot(rank_inputs, up_factor.astype(jnp.float32), precision=lax.Precision.HIGHEST)
        holder_down = (adapter_scale * jnp.dot(token_vectors.T, rank_outputs.astype(jnp.bfloat16), preferred_element_type=jnp.float32)).astype(jnp.bfloat16)
        holder_up = (adapter_scale * jnp.dot(rank_inputs.astype(jnp.bfloat16).T, gradient_rows, preferred_element_type=jnp.float32)).astype(jnp.bfloat16)
        return token_matrix, adapter_piece, holder_down, holder_up

    token_matrix, adapter_piece, down_gradient, up_gradient = lax.map(slot_grouped, adapter_index)
    adapter_tokens = jnp.zeros((TOKEN_TOTAL, VALUE_WIDTH), jnp.float32).at[token_matrix.reshape(-1)].add(adapter_piece.reshape(-1, VALUE_WIDTH), mode="drop")
    frozen_output = jnp.dot(tokens, value_weight, preferred_element_type=jnp.float32)
    mixed = (frozen_output + adapter_tokens).astype(jnp.bfloat16)
    return mixed, down_gradient, up_gradient
```

```python
import jax
import jax.numpy as jnp
from jax import lax
from jax.experimental import pallas as pl
from jax.experimental.pallas import tpu as pltpu
from jax.sharding import PartitionSpec as P

MESH = pl.DeviceIdType.MESH
PIECES = 4

adapter_scale = 2.0


def plain_body(tokens, output_gradient, value_weight, adapter_down, adapter_up, counts, holder_table):
    wide_count = lax.axis_size("wide")
    tok_rows = tokens.shape[0]
    resident_adapters = adapter_down.shape[0]
    all_adapters = resident_adapters * wide_count
    per_adapter = 2 * tok_rows // all_adapters
    row_counts = counts[0]
    group_ends = jnp.cumsum(row_counts)
    group_starts = group_ends - row_counts
    adapter_index = jnp.arange(all_adapters, dtype=jnp.int32)
    slot_table = (holder_table[None, :] == adapter_index[:, None]).astype(jnp.int32)
    slot_counts = jnp.dot(slot_table, row_counts)
    slot_starts = jnp.dot(slot_table, group_starts)
    offsets = jnp.arange(per_adapter, dtype=jnp.int32)
    valid = offsets[None, :] < slot_counts[:, None]
    source_rows = jnp.where(valid, slot_starts[:, None] + offsets[None, :], 0).reshape(-1)
    keep = valid.reshape(-1, 1)
    sent_tokens = jnp.where(
        keep, jnp.take(tokens, source_rows, axis=0), jnp.zeros((), tokens.dtype)
    )
    sent_grads = jnp.where(
        keep, jnp.take(output_gradient, source_rows, axis=0), jnp.zeros((), output_gradient.dtype)
    )
    sent_tokens = sent_tokens.reshape(wide_count, resident_adapters, per_adapter, tokens.shape[1])
    sent_grads = sent_grads.reshape(
        wide_count, resident_adapters, per_adapter, output_gradient.shape[1]
    )
    holder_tokens, holder_gradients = (
        lax.all_to_all(sent_tokens, "wide", split_axis=0, concat_axis=0, tiled=True),
        lax.all_to_all(sent_grads, "wide", split_axis=0, concat_axis=0, tiled=True),
    )
    down_part = jnp.einsum(
        "qopn,onx->qopx", holder_tokens, adapter_down, preferred_element_type=jnp.float32
    )
    up_piece = jnp.einsum(
        "gzme,zte->gzmt", holder_gradients, adapter_up, preferred_element_type=jnp.float32
    )
    rank_inputs, rank_outputs = lax.psum((down_part, up_piece), "narrow")
    in_low = rank_inputs.astype(jnp.bfloat16)
    out_low = rank_outputs.astype(jnp.bfloat16)
    down_gradient = (
        adapter_scale
        * jnp.einsum("wjkd,wjkr->jdr", holder_tokens, out_low, preferred_element_type=jnp.float32)
    ).astype(jnp.bfloat16)
    up_gradient = (
        adapter_scale
        * jnp.einsum("wjkr,wjkc->jrc", in_low, holder_gradients, preferred_element_type=jnp.float32)
    ).astype(jnp.bfloat16)
    token_pos = jnp.arange(tok_rows, dtype=jnp.int32)
    token_adapter = jnp.sum((group_ends[None, :] <= token_pos[:, None]).astype(jnp.int32), axis=1)
    token_table = (token_adapter[:, None] == adapter_index[None, :]).astype(jnp.int32)
    token_start = jnp.dot(token_table, group_starts)
    token_slot = jnp.dot(token_table, holder_table)
    back_rows = token_slot * per_adapter + token_pos - token_start
    base_part = jnp.dot(
        tokens,
        lax.all_gather(value_weight, "wide", axis=1, tiled=True),
        preferred_element_type=jnp.float32,
    )
    adapter_output = adapter_scale * jnp.einsum(
        "mpea,pai->mpei",
        rank_inputs,
        adapter_up.astype(jnp.float32),
        precision=lax.Precision.HIGHEST,
    )
    came_home = lax.all_to_all(adapter_output, "wide", split_axis=0, concat_axis=0, tiled=True)
    adapter_rows = jnp.take(
        came_home.reshape(all_adapters * per_adapter, came_home.shape[3]), back_rows, axis=0
    )
    combined_sum = lax.psum_scatter(base_part, "narrow", scatter_dimension=1, tiled=True)
    mixed = (combined_sum + adapter_rows).astype(jnp.bfloat16)
    return (mixed, down_gradient, up_gradient)


def exchange_kernel(
    weight, tokens, sent_tok, sent_grad,
    base, got_tok, got_grad,
    blocks, tok, acc, keep_own, keep_far, from_core, from_group,
    up_s, up_r, down_s, down_r, side_s, side_r, local, tok_s, tok_r, grad_s, grad_r, one_s, one_r,
):
    group = lax.axis_index("groups")
    me = lax.axis_index("wide")
    core = lax.axis_index("narrow")
    z, x = me // 2, me % 2
    depth = tok.shape[2]
    rows = depth // PIECES

    barrier = pltpu.get_barrier_semaphore()
    for k in range(1, 8):
        pl.semaphore_signal(barrier, inc=1, device_id={"wide": me ^ k}, device_id_type=MESH)
    pl.semaphore_signal(barrier, inc=1, device_id={"narrow": 1 - core}, device_id_type=MESH)
    pl.semaphore_signal(barrier, inc=1, device_id={"groups": 1 - group}, device_id_type=MESH)
    pl.semaphore_wait(barrier, 9)

    def step(first, slot, c, target, send, recv):
        there = blocks.at[slot, pl.ds(c * rows, rows)]
        here = weight.at[pl.ds(group * depth + c * rows, rows)] if first else there
        return pltpu.make_async_remote_copy(
            src_ref=here, dst_ref=there, send_sem=send, recv_sem=recv,
            device_id={"wide": target}, device_id_type=MESH,
        )

    for c in range(PIECES):
        @pl.when(z < 3)
        def _():
            step(True, me, c, me + 2, up_s.at[z, c], up_r.at[z, c]).start()

        @pl.when(z > 0)
        def _():
            step(True, me, c, me - 2, down_s.at[z, c], down_r.at[z, c]).start()

        step(True, me, c, me ^ 1, side_s.at[z, c], side_r.at[z, c]).start()

    far_tok = pltpu.make_async_remote_copy(
        src_ref=tokens.at[:, pl.ds((1 - group) * depth, depth)], dst_ref=tok.at[1],
        send_sem=one_s.at[0], recv_sem=one_r.at[0],
        device_id={"groups": 1 - group}, device_id_type=MESH,
    )
    far_tok.start()
    own = [
        pltpu.make_async_copy(
            weight.at[pl.ds(group * depth, depth)], blocks.at[me], local.at[0]),
        pltpu.make_async_copy(
            tokens.at[:, pl.ds(group * depth, depth)], tok.at[0], local.at[1]),
        pltpu.make_async_copy(sent_tok.at[me], got_tok.at[me], local.at[2]),
        pltpu.make_async_copy(sent_grad.at[me], got_grad.at[me], local.at[3]),
    ]
    for copy in own:
        copy.start()

    routed = []
    for k in range(1, 8):
        for src, dst, send, recv in (
            (sent_grad, got_grad, grad_s, grad_r), (sent_tok, got_tok, tok_s, tok_r)
        ):
            copy = pltpu.make_async_remote_copy(
                src_ref=src.at[me ^ k], dst_ref=dst.at[me],
                send_sem=send.at[k], recv_sem=recv.at[k],
                device_id={"wide": me ^ k}, device_id_type=MESH,
            )
            copy.start()
            routed.append(copy)

    for d in range(1, 4):
        for c in range(PIECES):
            @pl.when(z >= d)
            def _():
                at = z - d
                slot = 2 * at + x
                step(False, slot, c, me ^ 1, up_s.at[at, c], up_r.at[at, c]).wait_recv()

                @pl.when(z < 3)
                def _():
                    step(False, slot, c, me + 2, up_s.at[at, c], up_r.at[at, c]).start()

                step(False, slot, c, me ^ 1, side_s.at[at, c], side_r.at[at, c]).start()

            @pl.when(z + d < 4)
            def _():
                at = z + d
                slot = 2 * at + x
                step(False, slot, c, me ^ 1, down_s.at[at, c], down_r.at[at, c]).wait_recv()

                @pl.when(z > 0)
                def _():
                    step(False, slot, c, me - 2, down_s.at[at, c], down_r.at[at, c]).start()

                step(False, slot, c, me ^ 1, side_s.at[at, c], side_r.at[at, c]).start()

    for at in range(4):
        for c in range(PIECES):
            step(False, 2 * at + 1 - x, c, me ^ 1, side_s.at[at, c], side_r.at[at, c]).wait_recv()
    own[0].wait()
    own[1].wait()
    far_tok.wait_recv()

    both = tok[...].reshape(tok.shape[0] * tok.shape[1], depth)

    def column(w, carry):
        acc[w] = jnp.dot(both, blocks[w], preferred_element_type=jnp.float32)
        return carry

    lax.fori_loop(0, 8, column, 0)
    to_core = pltpu.make_async_remote_copy(
        src_ref=acc.at[pl.ds(4 * (1 - core), 4)], dst_ref=from_core,
        send_sem=one_s.at[1], recv_sem=one_r.at[1],
        device_id={"narrow": 1 - core}, device_id_type=MESH,
    )
    to_core.start()
    to_core.wait_recv()
    count = tok.shape[1]
    keep_far[...] = acc[pl.ds(4 * core, 4), count:] + from_core[:, count:]
    to_group = pltpu.make_async_remote_copy(
        src_ref=keep_far, dst_ref=from_group,
        send_sem=one_s.at[2], recv_sem=one_r.at[2],
        device_id={"groups": 1 - group}, device_id_type=MESH,
    )
    to_group.start()
    keep_own[...] = acc[pl.ds(4 * core, 4), :count] + from_core[:, :count]
    to_group.wait_recv()
    for w in range(4):
        base[:, w * 128 : (w + 1) * 128] = keep_own[w] + from_group[w]

    far_tok.wait_send()
    to_core.wait_send()
    to_group.wait_send()
    for at in range(4):
        for c in range(PIECES):
            step(False, 2 * at + x, c, me ^ 1, side_s.at[at, c], side_r.at[at, c]).wait_send()

            @pl.when((at <= z) & (z < 3))
            def _():
                step(False, 2 * at + x, c, me ^ 1, up_s.at[at, c], up_r.at[at, c]).wait_send()

            @pl.when((at >= z) & (z > 0))
            def _():
                step(False, 2 * at + x, c, me ^ 1, down_s.at[at, c], down_r.at[at, c]).wait_send()
    own[2].wait()
    own[3].wait()
    for copy in routed:
        copy.wait()


def exchange(weight, tokens, sent_tok, sent_grad):
    count, width = tokens.shape
    half = width // 2
    out_columns = weight.shape[1] * 4
    anywhere = pl.BlockSpec(memory_space=pl.ANY)
    dma = pltpu.SemaphoreType.DMA
    return pl.pallas_call(
        exchange_kernel,
        out_shape=(
            jax.ShapeDtypeStruct((count, out_columns), jnp.float32),
            jax.ShapeDtypeStruct(sent_tok.shape, sent_tok.dtype),
            jax.ShapeDtypeStruct(sent_grad.shape, sent_grad.dtype),
        ),
        in_specs=[anywhere] * 4,
        out_specs=(pl.BlockSpec(memory_space=pltpu.VMEM), anywhere, anywhere),
        scratch_shapes=[
            pltpu.VMEM((8, half, 128), jnp.bfloat16),
            pltpu.VMEM((2, count, half), jnp.bfloat16),
            pltpu.VMEM((8, 2 * count, 128), jnp.float32),
            pltpu.VMEM((4, count, 128), jnp.float32),
            pltpu.VMEM((4, count, 128), jnp.float32),
            pltpu.VMEM((4, 2 * count, 128), jnp.float32),
            pltpu.VMEM((4, count, 128), jnp.float32),
        ]
        + [dma((4, PIECES))] * 6
        + [dma((4,))]
        + [dma((8,))] * 4
        + [dma((3,))] * 2,
        compiler_params=pltpu.CompilerParams(
            collective_id=0, has_side_effects=True, vmem_limit_bytes=40 * 1024 * 1024
        ),
        cost_estimate=pl.CostEstimate(
            flops=2 * 512 * 2048 * 1024, bytes_accessed=40 * 1024 * 1024, transcendentals=0
        ),
    )(weight, tokens, sent_tok, sent_grad)


def over_cores(value):
    return value + lax.ppermute(value, "narrow", [(0, 1), (1, 0)])


def fused_body(
    tokens, output_gradient, value_weight, adapter_down, adapter_up, counts, holder_table
):
    exact = lax.Precision.HIGHEST
    wide_count = lax.axis_size("wide")
    tok_rows = tokens.shape[0]
    resident = adapter_down.shape[0]
    adapters = resident * wide_count
    per_adapter = 2 * tok_rows // adapters
    rank = adapter_down.shape[2]
    row_counts = counts[0]
    index = jnp.arange(adapters, dtype=jnp.int32)
    before = (index[None, :] < index[:, None]).astype(jnp.int32)
    starts = jnp.sum(before * row_counts[None, :], axis=1)
    slot_table = (holder_table[None, :] == index[:, None]).astype(jnp.int32)
    slot_counts = jnp.sum(slot_table * row_counts[None, :], axis=1)
    slot_starts = jnp.sum(slot_table * starts[None, :], axis=1)
    offset = jnp.arange(per_adapter, dtype=jnp.int32)
    position = jnp.arange(tok_rows, dtype=jnp.int32)
    source = jnp.where(
        offset[None, :] < slot_counts[:, None], slot_starts[:, None] + offset[None, :], -1
    )
    pick = source[:, :, None] == position[None, None, :]
    pick = pick.reshape(adapters * per_adapter, tok_rows)
    pick_low = pick.astype(jnp.bfloat16)
    sent_tok = jnp.dot(pick_low, tokens, preferred_element_type=jnp.bfloat16)
    sent_grad = jnp.dot(pick_low, output_gradient, preferred_element_type=jnp.bfloat16)
    all_up = lax.all_gather(adapter_up, "wide", axis=0, tiled=True)
    base, got_tok, got_grad = exchange(
        value_weight,
        tokens,
        sent_tok.reshape(wide_count, resident * per_adapter, -1),
        sent_grad.reshape(wide_count, resident * per_adapter, -1),
    )
    got_tok = got_tok.reshape(wide_count, resident, per_adapter, -1)
    got_grad = got_grad.reshape(wide_count, resident, per_adapter, -1)
    rank_in = over_cores(
        jnp.einsum("qopn,onx->qopx", got_tok, adapter_down, preferred_element_type=jnp.float32)
    )
    rank_out = over_cores(
        jnp.einsum("gzme,zte->gzmt", got_grad, adapter_up, preferred_element_type=jnp.float32)
    )
    home = lax.all_to_all(rank_in, "wide", split_axis=0, concat_axis=0, tiled=True)
    in_low = rank_in.astype(jnp.bfloat16)
    out_low = rank_out.astype(jnp.bfloat16)
    down_gradient = (
        adapter_scale
        * jnp.einsum("wjkd,wjkr->jdr", got_tok, out_low, preferred_element_type=jnp.float32)
    ).astype(jnp.bfloat16)
    up_gradient = (
        adapter_scale
        * jnp.einsum("wjkr,wjkc->jrc", in_low, got_grad, preferred_element_type=jnp.float32)
    ).astype(jnp.bfloat16)
    ranks = lax.dot_general(
        pick.astype(jnp.float32), home.reshape(adapters * per_adapter, rank),
        (((0,), (0,)), ((), ())), precision=exact,
    )
    owner = (position[:, None] >= slot_starts[None, :]) & (
        position[:, None] < (slot_starts + slot_counts)[None, :]
    )
    spread = jnp.where(owner[:, :, None], ranks[:, None, :], 0.0)
    lora = jnp.dot(
        spread.reshape(tok_rows, adapters * rank),
        all_up.reshape(adapters * rank, -1).astype(jnp.float32),
        precision=exact,
    )
    mixed = (base + adapter_scale * lora).astype(jnp.bfloat16)
    return (mixed, down_gradient, up_gradient)


def solution(mesh):
    in_specs = (
        P(("groups", "wide"), "narrow"),
        P(("groups", "wide"), "narrow"),
        P("narrow", "wide"),
        P(("groups", "wide"), "narrow", None),
        P(("groups", "wide"), None, "narrow"),
        P(("groups", "wide"), None),
        P("groups"),
    )
    out_specs = (
        P(("groups", "wide"), "narrow"),
        P(("groups", "wide"), "narrow", None),
        P(("groups", "wide"), None, "narrow"),
    )
    shape = mesh.shape
    small = (shape["groups"], shape["wide"], shape["narrow"]) == (2, 8, 2)
    body = fused_body if small else plain_body
    return jax.shard_map(body, mesh=mesh, in_specs=in_specs, out_specs=out_specs, check_vma=False)
```

```python
import jax
import jax.numpy as jnp
from jax import lax
from jax.experimental import pallas as pl
from jax.experimental.pallas import tpu as pltpu
from jax.sharding import PartitionSpec as P

MESH = pl.DeviceIdType.MESH
PIECES = 4

adapter_scale = 2.0


def plain_body(tokens, output_gradient, value_weight, adapter_down, adapter_up, counts, holder_table):
    wide_count = lax.axis_size("wide")
    tok_rows = tokens.shape[0]
    resident_adapters = adapter_down.shape[0]
    all_adapters = resident_adapters * wide_count
    per_adapter = 2 * tok_rows // all_adapters
    row_counts = counts[0]
    group_ends = jnp.cumsum(row_counts)
    group_starts = group_ends - row_counts
    adapter_index = jnp.arange(all_adapters, dtype=jnp.int32)
    slot_table = (holder_table[None, :] == adapter_index[:, None]).astype(jnp.int32)
    slot_counts = jnp.dot(slot_table, row_counts)
    slot_starts = jnp.dot(slot_table, group_starts)
    offsets = jnp.arange(per_adapter, dtype=jnp.int32)
    valid = offsets[None, :] < slot_counts[:, None]
    source_rows = jnp.where(valid, slot_starts[:, None] + offsets[None, :], 0).reshape(-1)
    keep = valid.reshape(-1, 1)
    sent_tokens = jnp.where(
        keep, jnp.take(tokens, source_rows, axis=0), jnp.zeros((), tokens.dtype)
    )
    sent_grads = jnp.where(
        keep, jnp.take(output_gradient, source_rows, axis=0), jnp.zeros((), output_gradient.dtype)
    )
    sent_tokens = sent_tokens.reshape(wide_count, resident_adapters, per_adapter, tokens.shape[1])
    sent_grads = sent_grads.reshape(
        wide_count, resident_adapters, per_adapter, output_gradient.shape[1]
    )
    holder_tokens, holder_gradients = (
        lax.all_to_all(sent_tokens, "wide", split_axis=0, concat_axis=0, tiled=True),
        lax.all_to_all(sent_grads, "wide", split_axis=0, concat_axis=0, tiled=True),
    )
    down_part = jnp.einsum(
        "qopn,onx->qopx", holder_tokens, adapter_down, preferred_element_type=jnp.float32
    )
    up_piece = jnp.einsum(
        "gzme,zte->gzmt", holder_gradients, adapter_up, preferred_element_type=jnp.float32
    )
    rank_inputs, rank_outputs = lax.psum((down_part, up_piece), "narrow")
    in_low = rank_inputs.astype(jnp.bfloat16)
    out_low = rank_outputs.astype(jnp.bfloat16)
    down_gradient = (
        adapter_scale
        * jnp.einsum("wjkd,wjkr->jdr", holder_tokens, out_low, preferred_element_type=jnp.float32)
    ).astype(jnp.bfloat16)
    up_gradient = (
        adapter_scale
        * jnp.einsum("wjkr,wjkc->jrc", in_low, holder_gradients, preferred_element_type=jnp.float32)
    ).astype(jnp.bfloat16)
    token_pos = jnp.arange(tok_rows, dtype=jnp.int32)
    token_adapter = jnp.sum((group_ends[None, :] <= token_pos[:, None]).astype(jnp.int32), axis=1)
    token_table = (token_adapter[:, None] == adapter_index[None, :]).astype(jnp.int32)
    token_start = jnp.dot(token_table, group_starts)
    token_slot = jnp.dot(token_table, holder_table)
    back_rows = token_slot * per_adapter + token_pos - token_start
    base_part = jnp.dot(
        tokens,
        lax.all_gather(value_weight, "wide", axis=1, tiled=True),
        preferred_element_type=jnp.float32,
    )
    adapter_output = adapter_scale * jnp.einsum(
        "mpea,pai->mpei",
        rank_inputs,
        adapter_up.astype(jnp.float32),
        precision=lax.Precision.HIGHEST,
    )
    came_home = lax.all_to_all(adapter_output, "wide", split_axis=0, concat_axis=0, tiled=True)
    adapter_rows = jnp.take(
        came_home.reshape(all_adapters * per_adapter, came_home.shape[3]), back_rows, axis=0
    )
    combined_sum = lax.psum_scatter(base_part, "narrow", scatter_dimension=1, tiled=True)
    mixed = (combined_sum + adapter_rows).astype(jnp.bfloat16)
    return (mixed, down_gradient, up_gradient)


def exchange_kernel(
    weight, tokens, sent_tok, sent_grad, down, up,
    base, down_grad, up_grad, home,
    blocks, tok, acc, keep_own, keep_far, from_core, from_group,
    got_tok, got_grad, part, far_part, low, landed,
    up_s, up_r, down_s, down_r, side_s, side_r, local, tok_s, tok_r, grad_s, grad_r, one_s, one_r,
    core_s, core_r, back_s, back_r,
):
    group = lax.axis_index("groups")
    me = lax.axis_index("wide")
    core = lax.axis_index("narrow")
    z, x = me // 2, me % 2
    depth = tok.shape[2]
    rows = depth // PIECES

    barrier = pltpu.get_barrier_semaphore()
    for k in range(1, 8):
        pl.semaphore_signal(barrier, inc=1, device_id={"wide": me ^ k}, device_id_type=MESH)
    pl.semaphore_signal(barrier, inc=1, device_id={"narrow": 1 - core}, device_id_type=MESH)
    pl.semaphore_signal(barrier, inc=1, device_id={"groups": 1 - group}, device_id_type=MESH)
    pl.semaphore_wait(barrier, 9)

    def step(first, slot, c, target, send, recv):
        there = blocks.at[slot, pl.ds(c * rows, rows)]
        here = weight.at[pl.ds(group * depth + c * rows, rows)] if first else there
        return pltpu.make_async_remote_copy(
            src_ref=here, dst_ref=there, send_sem=send, recv_sem=recv,
            device_id={"wide": target}, device_id_type=MESH,
        )

    for c in range(PIECES):
        @pl.when(z < 3)
        def _():
            step(True, me, c, me + 2, up_s.at[z, c], up_r.at[z, c]).start()

        @pl.when(z > 0)
        def _():
            step(True, me, c, me - 2, down_s.at[z, c], down_r.at[z, c]).start()

        step(True, me, c, me ^ 1, side_s.at[z, c], side_r.at[z, c]).start()

    far_tok = pltpu.make_async_remote_copy(
        src_ref=tokens.at[:, pl.ds((1 - group) * depth, depth)], dst_ref=tok.at[1],
        send_sem=one_s.at[0], recv_sem=one_r.at[0],
        device_id={"groups": 1 - group}, device_id_type=MESH,
    )
    far_tok.start()
    own = [
        pltpu.make_async_copy(
            weight.at[pl.ds(group * depth, depth)], blocks.at[me], local.at[0]),
        pltpu.make_async_copy(
            tokens.at[:, pl.ds(group * depth, depth)], tok.at[0], local.at[1]),
        pltpu.make_async_copy(sent_tok.at[me], got_tok.at[me], local.at[2]),
        pltpu.make_async_copy(sent_grad.at[me], got_grad.at[me], local.at[3]),
    ]
    for copy in own:
        copy.start()

    def route(src, dst, send, recv, k):
        return pltpu.make_async_remote_copy(
            src_ref=src.at[me ^ k], dst_ref=dst.at[me],
            send_sem=send.at[k], recv_sem=recv.at[k],
            device_id={"wide": me ^ k}, device_id_type=MESH,
        )

    toks, grads = {}, {}
    for k in (1, 2, 3, 4, 5, 6, 7):
        grads[k] = route(sent_grad, got_grad, grad_s, grad_r, k)
        grads[k].start()
    for k in (1, 2, 3):
        toks[k] = route(sent_tok, got_tok, tok_s, tok_r, k)
        toks[k].start()

    for d in range(1, 3):
        for c in range(PIECES):
            @pl.when(z >= d)
            def _():
                at = z - d
                slot = 2 * at + x
                step(False, slot, c, me ^ 1, up_s.at[at, c], up_r.at[at, c]).wait_recv()

                @pl.when(z < 3)
                def _():
                    step(False, slot, c, me + 2, up_s.at[at, c], up_r.at[at, c]).start()

                step(False, slot, c, me ^ 1, side_s.at[at, c], side_r.at[at, c]).start()

            @pl.when(z + d < 4)
            def _():
                at = z + d
                slot = 2 * at + x
                step(False, slot, c, me ^ 1, down_s.at[at, c], down_r.at[at, c]).wait_recv()

                @pl.when(z > 0)
                def _():
                    step(False, slot, c, me - 2, down_s.at[at, c], down_r.at[at, c]).start()

                step(False, slot, c, me ^ 1, side_s.at[at, c], side_r.at[at, c]).start()

    for k in (4, 5, 6, 7):
        toks[k] = route(sent_tok, got_tok, tok_s, tok_r, k)
        toks[k].start()

    for d in range(3, 4):
        for c in range(PIECES):
            @pl.when(z >= d)
            def _():
                at = z - d
                slot = 2 * at + x
                step(False, slot, c, me ^ 1, up_s.at[at, c], up_r.at[at, c]).wait_recv()

                @pl.when(z < 3)
                def _():
                    step(False, slot, c, me + 2, up_s.at[at, c], up_r.at[at, c]).start()

                step(False, slot, c, me ^ 1, side_s.at[at, c], side_r.at[at, c]).start()

            @pl.when(z + d < 4)
            def _():
                at = z + d
                slot = 2 * at + x
                step(False, slot, c, me ^ 1, down_s.at[at, c], down_r.at[at, c]).wait_recv()

                @pl.when(z > 0)
                def _():
                    step(False, slot, c, me - 2, down_s.at[at, c], down_r.at[at, c]).start()

                step(False, slot, c, me ^ 1, side_s.at[at, c], side_r.at[at, c]).start()


    for at in range(4):
        for c in range(PIECES):
            step(False, 2 * at + 1 - x, c, me ^ 1, side_s.at[at, c], side_r.at[at, c]).wait_recv()
    own[0].wait()
    own[1].wait()
    far_tok.wait_recv()

    both = tok[...].reshape(tok.shape[0] * tok.shape[1], depth)

    def column(w, carry):
        acc[w] = jnp.dot(both, blocks[w], preferred_element_type=jnp.float32)
        return carry

    lax.fori_loop(0, 8, column, 0)
    to_core = pltpu.make_async_remote_copy(
        src_ref=acc.at[pl.ds(4 * (1 - core), 4)], dst_ref=from_core,
        send_sem=one_s.at[1], recv_sem=one_r.at[1],
        device_id={"narrow": 1 - core}, device_id_type=MESH,
    )
    to_core.start()
    to_core.wait_recv()
    count = tok.shape[1]
    keep_far[...] = acc[pl.ds(4 * core, 4), count:] + from_core[:, count:]
    to_group = pltpu.make_async_remote_copy(
        src_ref=keep_far, dst_ref=from_group,
        send_sem=one_s.at[2], recv_sem=one_r.at[2],
        device_id={"groups": 1 - group}, device_id_type=MESH,
    )
    to_group.start()
    keep_own[...] = acc[pl.ds(4 * core, 4), :count] + from_core[:, :count]
    to_group.wait_recv()
    for w in range(4):
        base[:, w * 128 : (w + 1) * 128] = keep_own[w] + from_group[w]

    far_tok.wait_send()
    to_core.wait_send()
    to_group.wait_send()
    for at in range(4):
        for c in range(PIECES):
            step(False, 2 * at + x, c, me ^ 1, side_s.at[at, c], side_r.at[at, c]).wait_send()

            @pl.when((at <= z) & (z < 3))
            def _():
                step(False, 2 * at + x, c, me ^ 1, up_s.at[at, c], up_r.at[at, c]).wait_send()

            @pl.when((at >= z) & (z > 0))
            def _():
                step(False, 2 * at + x, c, me ^ 1, down_s.at[at, c], down_r.at[at, c]).wait_send()
    slots = got_tok.shape[1]
    width = part.shape[3]
    row = lax.broadcasted_iota(jnp.int32, (slots, width), 0) // (slots // 2)
    column_half = lax.broadcasted_iota(jnp.int32, (slots, width), 1) // (width // 2)
    matches = row == column_half
    by_row = (((1,), (1,)), ((), ()))
    shares = []
    for k in range(8):
        if k == 0:
            own[2].wait()
            own[3].wait()
        else:
            grads[k].wait_recv()
            toks[k].wait_recv()
        at = me ^ k
        part[at, 0] = lax.dot_general(
            got_tok[at], down[...], by_row, preferred_element_type=jnp.float32)
        part[at, 1] = lax.dot_general(
            got_grad[at], up[...], by_row, preferred_element_type=jnp.float32)
        share = pltpu.make_async_remote_copy(
            src_ref=part.at[at], dst_ref=far_part.at[at],
            send_sem=core_s.at[k], recv_sem=core_r.at[k],
            device_id={"narrow": 1 - core}, device_id_type=MESH,
        )
        share.start()
        shares.append(share)
    backs = []
    for k in range(8):
        at = me ^ k
        shares[k].wait()
        total_in = jnp.where(matches, part[at, 0] + far_part[at, 0], 0.0)
        total_out = jnp.where(matches, part[at, 1] + far_part[at, 1], 0.0)
        low[0, at] = total_in.astype(jnp.bfloat16)
        low[1, at] = total_out.astype(jnp.bfloat16)
        if k == 0:
            home[at] = total_in
        else:
            part[at, 0] = total_in
            back = pltpu.make_async_remote_copy(
                src_ref=part.at[at, 0], dst_ref=landed.at[me],
                send_sem=back_s.at[k], recv_sem=back_r.at[k],
                device_id={"wide": at}, device_id_type=MESH,
            )
            back.start()
            backs.append(back)
    by_slot = (((0,), (0,)), ((), ()))
    in_low = low[0].reshape(8 * slots, width)
    out_low = low[1].reshape(8 * slots, width)
    tile = up.shape[1]

    def columns(i, carry):
        at = pl.ds(pl.multiple_of(i * tile, tile), tile)
        down_grad[:, at] = (
            adapter_scale
            * lax.dot_general(
                out_low, got_tok[:, :, at].reshape(8 * slots, tile), by_slot,
                preferred_element_type=jnp.float32)
        ).astype(jnp.bfloat16)
        return carry

    lax.fori_loop(0, down.shape[1] // tile, columns, 0)
    up_grad[...] = (
        adapter_scale
        * lax.dot_general(
            in_low, got_grad[...].reshape(8 * slots, tile), by_slot,
            preferred_element_type=jnp.float32)
    ).astype(jnp.bfloat16)
    for k in range(1, 8):
        backs[k - 1].wait()
        home[me ^ k] = landed[me ^ k]
        toks[k].wait_send()
        grads[k].wait_send()


def exchange(weight, tokens, sent_tok, sent_grad, down, up):
    count, width = tokens.shape
    half = width // 2
    out_columns = weight.shape[1] * 4
    anywhere = pl.BlockSpec(memory_space=pl.ANY)
    vmem = pl.BlockSpec(memory_space=pltpu.VMEM)
    dma = pltpu.SemaphoreType.DMA
    slots, ranks = sent_tok.shape[1], down.shape[0]
    return pl.pallas_call(
        exchange_kernel,
        out_shape=(
            jax.ShapeDtypeStruct((count, out_columns), jnp.float32),
            jax.ShapeDtypeStruct(down.shape, down.dtype),
            jax.ShapeDtypeStruct(up.shape, up.dtype),
            jax.ShapeDtypeStruct((8, slots, ranks), jnp.float32),
        ),
        in_specs=[anywhere] * 4 + [vmem] * 2,
        out_specs=(vmem,) * 4,
        scratch_shapes=[
            pltpu.VMEM((8, half, 128), jnp.bfloat16),
            pltpu.VMEM((2, count, half), jnp.bfloat16),
            pltpu.VMEM((8, 2 * count, 128), jnp.float32),
            pltpu.VMEM((4, count, 128), jnp.float32),
            pltpu.VMEM((4, count, 128), jnp.float32),
            pltpu.VMEM((4, 2 * count, 128), jnp.float32),
            pltpu.VMEM((4, count, 128), jnp.float32),
            pltpu.VMEM(sent_tok.shape, jnp.bfloat16),
            pltpu.VMEM(sent_grad.shape, jnp.bfloat16),
            pltpu.VMEM((8, 2, slots, ranks), jnp.float32),
            pltpu.VMEM((8, 2, slots, ranks), jnp.float32),
            pltpu.VMEM((2, 8, slots, ranks), jnp.bfloat16),
            pltpu.VMEM((8, slots, ranks), jnp.float32),
        ]
        + [dma((4, PIECES))] * 6
        + [dma((4,))]
        + [dma((8,))] * 4
        + [dma((3,))] * 2
        + [dma((8,))] * 4,
        compiler_params=pltpu.CompilerParams(
            collective_id=0, has_side_effects=True, vmem_limit_bytes=40 * 1024 * 1024
        ),
        cost_estimate=pl.CostEstimate(
            flops=2 * 512 * 2048 * 1024, bytes_accessed=40 * 1024 * 1024, transcendentals=0
        ),
    )(weight, tokens, sent_tok, sent_grad, down, up)


def fused_body(
    tokens, output_gradient, value_weight, adapter_down, adapter_up, counts, holder_table
):
    exact = lax.Precision.HIGHEST
    wide_count = lax.axis_size("wide")
    tok_rows = tokens.shape[0]
    resident = adapter_down.shape[0]
    adapters = resident * wide_count
    per_adapter = 2 * tok_rows // adapters
    rank = adapter_down.shape[2]
    row_counts = counts[0]
    index = jnp.arange(adapters, dtype=jnp.int32)
    before = (index[None, :] < index[:, None]).astype(jnp.int32)
    starts = jnp.sum(before * row_counts[None, :], axis=1)
    slot_table = (holder_table[None, :] == index[:, None]).astype(jnp.int32)
    slot_counts = jnp.sum(slot_table * row_counts[None, :], axis=1)
    slot_starts = jnp.sum(slot_table * starts[None, :], axis=1)
    offset = jnp.arange(per_adapter, dtype=jnp.int32)
    position = jnp.arange(tok_rows, dtype=jnp.int32)
    source = jnp.where(
        offset[None, :] < slot_counts[:, None], slot_starts[:, None] + offset[None, :], -1
    )
    pick = source[:, :, None] == position[None, None, :]
    pick = pick.reshape(adapters * per_adapter, tok_rows)
    pick_low = pick.astype(jnp.bfloat16)
    sent_tok = jnp.dot(pick_low, tokens, preferred_element_type=jnp.bfloat16)
    sent_grad = jnp.dot(pick_low, output_gradient, preferred_element_type=jnp.bfloat16)
    all_up = lax.all_gather(adapter_up, "wide", axis=0, tiled=True)
    base, down_gradient, up_gradient, home = exchange(
        value_weight,
        tokens,
        sent_tok.reshape(wide_count, resident * per_adapter, -1),
        sent_grad.reshape(wide_count, resident * per_adapter, -1),
        jnp.swapaxes(adapter_down, 1, 2).reshape(resident * rank, -1),
        adapter_up.reshape(resident * rank, -1),
    )
    down_gradient = jnp.swapaxes(down_gradient.reshape(resident, rank, -1), 1, 2)
    up_gradient = up_gradient.reshape(adapter_up.shape)
    ranks = lax.dot_general(
        pick.astype(jnp.float32), home.reshape(adapters * per_adapter, resident * rank),
        (((0,), (0,)), ((), ())), precision=exact,
    )
    owner = jnp.any(pick.reshape(wide_count, resident * per_adapter, tok_rows), axis=1).T
    spread = jnp.where(owner[:, :, None], ranks[:, None, :], 0.0)
    lora = jnp.dot(
        spread.reshape(tok_rows, adapters * rank),
        all_up.reshape(adapters * rank, -1).astype(jnp.float32),
        precision=exact,
    )
    mixed = (base + adapter_scale * lora).astype(jnp.bfloat16)
    return (mixed, down_gradient, up_gradient)


def solution(mesh):
    in_specs = (
        P(("groups", "wide"), "narrow"),
        P(("groups", "wide"), "narrow"),
        P("narrow", "wide"),
        P(("groups", "wide"), "narrow", None),
        P(("groups", "wide"), None, "narrow"),
        P(("groups", "wide"), None),
        P("groups"),
    )
    out_specs = (
        P(("groups", "wide"), "narrow"),
        P(("groups", "wide"), "narrow", None),
        P(("groups", "wide"), None, "narrow"),
    )
    shape = mesh.shape
    small = (shape["groups"], shape["wide"], shape["narrow"]) == (2, 8, 2)
    body = fused_body if small else plain_body
    return jax.shard_map(body, mesh=mesh, in_specs=in_specs, out_specs=out_specs, check_vma=False)
```

```python
import jax
import jax.numpy as jnp
from jax import lax
from jax.experimental import pallas as pl
from jax.experimental.pallas import tpu as pltpu
from jax.sharding import PartitionSpec as P

MESH = pl.DeviceIdType.MESH
PIECES = 2

adapter_scale = 2.0


def plain_body(tokens, output_gradient, value_weight, adapter_down, adapter_up, counts, holder_table):
    wide_count = lax.axis_size("wide")
    tok_rows = tokens.shape[0]
    resident_adapters = adapter_down.shape[0]
    all_adapters = resident_adapters * wide_count
    per_adapter = 2 * tok_rows // all_adapters
    row_counts = counts[0]
    group_ends = jnp.cumsum(row_counts)
    group_starts = group_ends - row_counts
    adapter_index = jnp.arange(all_adapters, dtype=jnp.int32)
    slot_table = (holder_table[None, :] == adapter_index[:, None]).astype(jnp.int32)
    slot_counts = jnp.dot(slot_table, row_counts)
    slot_starts = jnp.dot(slot_table, group_starts)
    offsets = jnp.arange(per_adapter, dtype=jnp.int32)
    valid = offsets[None, :] < slot_counts[:, None]
    source_rows = jnp.where(valid, slot_starts[:, None] + offsets[None, :], 0).reshape(-1)
    keep = valid.reshape(-1, 1)
    sent_tokens = jnp.where(
        keep, jnp.take(tokens, source_rows, axis=0), jnp.zeros((), tokens.dtype)
    )
    sent_grads = jnp.where(
        keep, jnp.take(output_gradient, source_rows, axis=0), jnp.zeros((), output_gradient.dtype)
    )
    sent_tokens = sent_tokens.reshape(wide_count, resident_adapters, per_adapter, tokens.shape[1])
    sent_grads = sent_grads.reshape(
        wide_count, resident_adapters, per_adapter, output_gradient.shape[1]
    )
    holder_tokens, holder_gradients = (
        lax.all_to_all(sent_tokens, "wide", split_axis=0, concat_axis=0, tiled=True),
        lax.all_to_all(sent_grads, "wide", split_axis=0, concat_axis=0, tiled=True),
    )
    down_part = jnp.einsum(
        "qopn,onx->qopx", holder_tokens, adapter_down, preferred_element_type=jnp.float32
    )
    up_piece = jnp.einsum(
        "gzme,zte->gzmt", holder_gradients, adapter_up, preferred_element_type=jnp.float32
    )
    rank_inputs, rank_outputs = lax.psum((down_part, up_piece), "narrow")
    in_low = rank_inputs.astype(jnp.bfloat16)
    out_low = rank_outputs.astype(jnp.bfloat16)
    down_gradient = (
        adapter_scale
        * jnp.einsum("wjkd,wjkr->jdr", holder_tokens, out_low, preferred_element_type=jnp.float32)
    ).astype(jnp.bfloat16)
    up_gradient = (
        adapter_scale
        * jnp.einsum("wjkr,wjkc->jrc", in_low, holder_gradients, preferred_element_type=jnp.float32)
    ).astype(jnp.bfloat16)
    token_pos = jnp.arange(tok_rows, dtype=jnp.int32)
    token_adapter = jnp.sum((group_ends[None, :] <= token_pos[:, None]).astype(jnp.int32), axis=1)
    token_table = (token_adapter[:, None] == adapter_index[None, :]).astype(jnp.int32)
    token_start = jnp.dot(token_table, group_starts)
    token_slot = jnp.dot(token_table, holder_table)
    back_rows = token_slot * per_adapter + token_pos - token_start
    base_part = jnp.dot(
        tokens,
        lax.all_gather(value_weight, "wide", axis=1, tiled=True),
        preferred_element_type=jnp.float32,
    )
    adapter_output = adapter_scale * jnp.einsum(
        "mpea,pai->mpei",
        rank_inputs,
        adapter_up.astype(jnp.float32),
        precision=lax.Precision.HIGHEST,
    )
    came_home = lax.all_to_all(adapter_output, "wide", split_axis=0, concat_axis=0, tiled=True)
    adapter_rows = jnp.take(
        came_home.reshape(all_adapters * per_adapter, came_home.shape[3]), back_rows, axis=0
    )
    combined_sum = lax.psum_scatter(base_part, "narrow", scatter_dimension=1, tiled=True)
    mixed = (combined_sum + adapter_rows).astype(jnp.bfloat16)
    return (mixed, down_gradient, up_gradient)


def exchange_kernel(
    weight, tokens, sent_tok, sent_grad, down, up,
    base, down_grad, up_grad, home,
    blocks, tok, acc, keep_own, keep_far, from_core, from_group,
    got_tok, got_grad, part, far_part, low, landed,
    up_s, up_r, down_s, down_r, side_s, side_r, local, tok_s, tok_r, grad_s, grad_r, one_s, one_r,
    core_s, core_r, back_s, back_r,
):
    group = lax.axis_index("groups")
    me = lax.axis_index("wide")
    core = lax.axis_index("narrow")
    z, x = me // 2, me % 2
    depth = tok.shape[2]
    rows = depth // PIECES

    barrier = pltpu.get_barrier_semaphore()
    for k in range(1, 8):
        pl.semaphore_signal(barrier, inc=1, device_id={"wide": me ^ k}, device_id_type=MESH)
    pl.semaphore_signal(barrier, inc=1, device_id={"narrow": 1 - core}, device_id_type=MESH)
    pl.semaphore_signal(barrier, inc=1, device_id={"groups": 1 - group}, device_id_type=MESH)
    pl.semaphore_wait(barrier, 9)

    def step(first, slot, c, target, send, recv):
        there = blocks.at[slot, pl.ds(c * rows, rows)]
        here = weight.at[pl.ds(group * depth + c * rows, rows)] if first else there
        return pltpu.make_async_remote_copy(
            src_ref=here, dst_ref=there, send_sem=send, recv_sem=recv,
            device_id={"wide": target}, device_id_type=MESH,
        )

    for c in range(PIECES):
        @pl.when(z < 3)
        def _():
            step(True, me, c, me + 2, up_s.at[z, c], up_r.at[z, c]).start()

        @pl.when(z > 0)
        def _():
            step(True, me, c, me - 2, down_s.at[z, c], down_r.at[z, c]).start()

        step(True, me, c, me ^ 1, side_s.at[z, c], side_r.at[z, c]).start()

    far_tok = pltpu.make_async_remote_copy(
        src_ref=tokens.at[:, pl.ds((1 - group) * depth, depth)], dst_ref=tok.at[1],
        send_sem=one_s.at[0], recv_sem=one_r.at[0],
        device_id={"groups": 1 - group}, device_id_type=MESH,
    )
    far_tok.start()
    own = [
        pltpu.make_async_copy(
            weight.at[pl.ds(group * depth, depth)], blocks.at[me], local.at[0]),
        pltpu.make_async_copy(
            tokens.at[:, pl.ds(group * depth, depth)], tok.at[0], local.at[1]),
        pltpu.make_async_copy(sent_tok.at[me], got_tok.at[me], local.at[2]),
        pltpu.make_async_copy(sent_grad.at[me], got_grad.at[me], local.at[3]),
    ]
    for copy in own:
        copy.start()

    def route(src, dst, send, recv, k):
        return pltpu.make_async_remote_copy(
            src_ref=src.at[me ^ k], dst_ref=dst.at[me],
            send_sem=send.at[k], recv_sem=recv.at[k],
            device_id={"wide": me ^ k}, device_id_type=MESH,
        )

    toks, grads = {}, {}
    for k in (1, 2, 3):
        toks[k] = route(sent_tok, got_tok, tok_s, tok_r, k)
        toks[k].start()

    for d in range(1, 3):
        for c in range(PIECES):
            @pl.when(z >= d)
            def _():
                at = z - d
                slot = 2 * at + x
                step(False, slot, c, me ^ 1, up_s.at[at, c], up_r.at[at, c]).wait_recv()

                @pl.when(z < 3)
                def _():
                    step(False, slot, c, me + 2, up_s.at[at, c], up_r.at[at, c]).start()

                step(False, slot, c, me ^ 1, side_s.at[at, c], side_r.at[at, c]).start()

            @pl.when(z + d < 4)
            def _():
                at = z + d
                slot = 2 * at + x
                step(False, slot, c, me ^ 1, down_s.at[at, c], down_r.at[at, c]).wait_recv()

                @pl.when(z > 0)
                def _():
                    step(False, slot, c, me - 2, down_s.at[at, c], down_r.at[at, c]).start()

                step(False, slot, c, me ^ 1, side_s.at[at, c], side_r.at[at, c]).start()

    for k in (4, 5, 6, 7):
        toks[k] = route(sent_tok, got_tok, tok_s, tok_r, k)
        toks[k].start()
    for k in (1, 2, 3, 4, 5, 6, 7):
        grads[k] = route(sent_grad, got_grad, grad_s, grad_r, k)
        grads[k].start()

    for d in range(3, 4):
        for c in range(PIECES):
            @pl.when(z >= d)
            def _():
                at = z - d
                slot = 2 * at + x
                step(False, slot, c, me ^ 1, up_s.at[at, c], up_r.at[at, c]).wait_recv()

                @pl.when(z < 3)
                def _():
                    step(False, slot, c, me + 2, up_s.at[at, c], up_r.at[at, c]).start()

                step(False, slot, c, me ^ 1, side_s.at[at, c], side_r.at[at, c]).start()

            @pl.when(z + d < 4)
            def _():
                at = z + d
                slot = 2 * at + x
                step(False, slot, c, me ^ 1, down_s.at[at, c], down_r.at[at, c]).wait_recv()

                @pl.when(z > 0)
                def _():
                    step(False, slot, c, me - 2, down_s.at[at, c], down_r.at[at, c]).start()

                step(False, slot, c, me ^ 1, side_s.at[at, c], side_r.at[at, c]).start()


    for at in range(4):
        for c in range(PIECES):
            step(False, 2 * at + 1 - x, c, me ^ 1, side_s.at[at, c], side_r.at[at, c]).wait_recv()
    own[0].wait()
    own[1].wait()
    far_tok.wait_recv()

    both = tok[...].reshape(tok.shape[0] * tok.shape[1], depth)

    def column(w, carry):
        acc[w] = jnp.dot(both, blocks[w], preferred_element_type=jnp.float32)
        return carry

    lax.fori_loop(0, 8, column, 0)
    to_core = pltpu.make_async_remote_copy(
        src_ref=acc.at[pl.ds(4 * (1 - core), 4)], dst_ref=from_core,
        send_sem=one_s.at[1], recv_sem=one_r.at[1],
        device_id={"narrow": 1 - core}, device_id_type=MESH,
    )
    to_core.start()
    to_core.wait_recv()
    count = tok.shape[1]
    keep_far[...] = acc[pl.ds(4 * core, 4), count:] + from_core[:, count:]
    to_group = pltpu.make_async_remote_copy(
        src_ref=keep_far, dst_ref=from_group,
        send_sem=one_s.at[2], recv_sem=one_r.at[2],
        device_id={"groups": 1 - group}, device_id_type=MESH,
    )
    to_group.start()
    keep_own[...] = acc[pl.ds(4 * core, 4), :count] + from_core[:, :count]
    to_group.wait_recv()
    for w in range(4):
        base[:, w * 128 : (w + 1) * 128] = keep_own[w] + from_group[w]

    far_tok.wait_send()
    to_core.wait_send()
    to_group.wait_send()
    for at in range(4):
        for c in range(PIECES):
            step(False, 2 * at + x, c, me ^ 1, side_s.at[at, c], side_r.at[at, c]).wait_send()

            @pl.when((at <= z) & (z < 3))
            def _():
                step(False, 2 * at + x, c, me ^ 1, up_s.at[at, c], up_r.at[at, c]).wait_send()

            @pl.when((at >= z) & (z > 0))
            def _():
                step(False, 2 * at + x, c, me ^ 1, down_s.at[at, c], down_r.at[at, c]).wait_send()
    slots = got_tok.shape[1]
    width = part.shape[3]
    row = lax.broadcasted_iota(jnp.int32, (slots, width), 0) // (slots // 2)
    column_half = lax.broadcasted_iota(jnp.int32, (slots, width), 1) // (width // 2)
    matches = row == column_half
    by_row = (((1,), (1,)), ((), ()))
    shares = []
    for k in range(8):
        if k == 0:
            own[2].wait()
            own[3].wait()
        else:
            grads[k].wait_recv()
            toks[k].wait_recv()
        at = me ^ k
        part[at, 0] = lax.dot_general(
            got_tok[at], down[...], by_row, preferred_element_type=jnp.float32)
        part[at, 1] = lax.dot_general(
            got_grad[at], up[...], by_row, preferred_element_type=jnp.float32)
        share = pltpu.make_async_remote_copy(
            src_ref=part.at[at], dst_ref=far_part.at[at],
            send_sem=core_s.at[k], recv_sem=core_r.at[k],
            device_id={"narrow": 1 - core}, device_id_type=MESH,
        )
        share.start()
        shares.append(share)
    backs = []
    for k in range(8):
        at = me ^ k
        shares[k].wait()
        total_in = jnp.where(matches, part[at, 0] + far_part[at, 0], 0.0)
        total_out = jnp.where(matches, part[at, 1] + far_part[at, 1], 0.0)
        low[0, at] = total_in.astype(jnp.bfloat16)
        low[1, at] = total_out.astype(jnp.bfloat16)
        if k == 0:
            home[at] = total_in
        else:
            part[at, 0] = total_in
            back = pltpu.make_async_remote_copy(
                src_ref=part.at[at, 0], dst_ref=landed.at[me],
                send_sem=back_s.at[k], recv_sem=back_r.at[k],
                device_id={"wide": at}, device_id_type=MESH,
            )
            back.start()
            backs.append(back)
    by_slot = (((0,), (0,)), ((), ()))
    in_low = low[0].reshape(8 * slots, width)
    out_low = low[1].reshape(8 * slots, width)
    tile = up.shape[1]

    def columns(i, carry):
        at = pl.ds(pl.multiple_of(i * tile, tile), tile)
        down_grad[:, at] = (
            adapter_scale
            * lax.dot_general(
                out_low, got_tok[:, :, at].reshape(8 * slots, tile), by_slot,
                preferred_element_type=jnp.float32)
        ).astype(jnp.bfloat16)
        return carry

    lax.fori_loop(0, down.shape[1] // tile, columns, 0)
    up_grad[...] = (
        adapter_scale
        * lax.dot_general(
            in_low, got_grad[...].reshape(8 * slots, tile), by_slot,
            preferred_element_type=jnp.float32)
    ).astype(jnp.bfloat16)
    for k in range(1, 8):
        backs[k - 1].wait()
        home[me ^ k] = landed[me ^ k]
        toks[k].wait_send()
        grads[k].wait_send()


def exchange(weight, tokens, sent_tok, sent_grad, down, up):
    count, width = tokens.shape
    half = width // 2
    out_columns = weight.shape[1] * 4
    anywhere = pl.BlockSpec(memory_space=pl.ANY)
    vmem = pl.BlockSpec(memory_space=pltpu.VMEM)
    dma = pltpu.SemaphoreType.DMA
    slots, ranks = sent_tok.shape[1], down.shape[0]
    return pl.pallas_call(
        exchange_kernel,
        out_shape=(
            jax.ShapeDtypeStruct((count, out_columns), jnp.float32),
            jax.ShapeDtypeStruct(down.shape, down.dtype),
            jax.ShapeDtypeStruct(up.shape, up.dtype),
            jax.ShapeDtypeStruct((8, slots, ranks), jnp.float32),
        ),
        in_specs=[anywhere] * 4 + [vmem] * 2,
        out_specs=(vmem,) * 4,
        scratch_shapes=[
            pltpu.VMEM((8, half, 128), jnp.bfloat16),
            pltpu.VMEM((2, count, half), jnp.bfloat16),
            pltpu.VMEM((8, 2 * count, 128), jnp.float32),
            pltpu.VMEM((4, count, 128), jnp.float32),
            pltpu.VMEM((4, count, 128), jnp.float32),
            pltpu.VMEM((4, 2 * count, 128), jnp.float32),
            pltpu.VMEM((4, count, 128), jnp.float32),
            pltpu.VMEM(sent_tok.shape, jnp.bfloat16),
            pltpu.VMEM(sent_grad.shape, jnp.bfloat16),
            pltpu.VMEM((8, 2, slots, ranks), jnp.float32),
            pltpu.VMEM((8, 2, slots, ranks), jnp.float32),
            pltpu.VMEM((2, 8, slots, ranks), jnp.bfloat16),
            pltpu.VMEM((8, slots, ranks), jnp.float32),
        ]
        + [dma((4, PIECES))] * 6
        + [dma((4,))]
        + [dma((8,))] * 4
        + [dma((3,))] * 2
        + [dma((8,))] * 4,
        compiler_params=pltpu.CompilerParams(
            collective_id=0, has_side_effects=True, vmem_limit_bytes=40 * 1024 * 1024
        ),
        cost_estimate=pl.CostEstimate(
            flops=2 * 512 * 2048 * 1024, bytes_accessed=40 * 1024 * 1024, transcendentals=0
        ),
    )(weight, tokens, sent_tok, sent_grad, down, up)


def fused_body(
    tokens, output_gradient, value_weight, adapter_down, adapter_up, counts, holder_table
):
    exact = lax.Precision.HIGHEST
    wide_count = lax.axis_size("wide")
    tok_rows = tokens.shape[0]
    resident = adapter_down.shape[0]
    adapters = resident * wide_count
    per_adapter = 2 * tok_rows // adapters
    rank = adapter_down.shape[2]
    row_counts = counts[0]
    index = jnp.arange(adapters, dtype=jnp.int32)
    before = (index[None, :] < index[:, None]).astype(jnp.int32)
    starts = jnp.sum(before * row_counts[None, :], axis=1)
    slot_table = (holder_table[None, :] == index[:, None]).astype(jnp.int32)
    slot_counts = jnp.sum(slot_table * row_counts[None, :], axis=1)
    slot_starts = jnp.sum(slot_table * starts[None, :], axis=1)
    offset = jnp.arange(per_adapter, dtype=jnp.int32)
    position = jnp.arange(tok_rows, dtype=jnp.int32)
    source = jnp.where(
        offset[None, :] < slot_counts[:, None], slot_starts[:, None] + offset[None, :], -1
    )
    pick = source[:, :, None] == position[None, None, :]
    pick = pick.reshape(adapters * per_adapter, tok_rows)
    pick_low = pick.astype(jnp.bfloat16)
    sent_tok = jnp.dot(pick_low, tokens, preferred_element_type=jnp.bfloat16)
    sent_grad = jnp.dot(pick_low, output_gradient, preferred_element_type=jnp.bfloat16)
    all_up = lax.all_gather(adapter_up, "wide", axis=0, tiled=True)
    base, down_gradient, up_gradient, home = exchange(
        value_weight,
        tokens,
        sent_tok.reshape(wide_count, resident * per_adapter, -1),
        sent_grad.reshape(wide_count, resident * per_adapter, -1),
        jnp.swapaxes(adapter_down, 1, 2).reshape(resident * rank, -1),
        adapter_up.reshape(resident * rank, -1),
    )
    down_gradient = jnp.swapaxes(down_gradient.reshape(resident, rank, -1), 1, 2)
    up_gradient = up_gradient.reshape(adapter_up.shape)
    ranks = lax.dot_general(
        pick.astype(jnp.float32), home.reshape(adapters * per_adapter, resident * rank),
        (((0,), (0,)), ((), ())), precision=exact,
    )
    owner = jnp.any(pick.reshape(wide_count, resident * per_adapter, tok_rows), axis=1).T
    spread = jnp.where(owner[:, :, None], ranks[:, None, :], 0.0)
    lora = jnp.dot(
        spread.reshape(tok_rows, adapters * rank),
        all_up.reshape(adapters * rank, -1).astype(jnp.float32),
        precision=exact,
    )
    mixed = (base + adapter_scale * lora).astype(jnp.bfloat16)
    return (mixed, down_gradient, up_gradient)


def solution(mesh):
    in_specs = (
        P(("groups", "wide"), "narrow"),
        P(("groups", "wide"), "narrow"),
        P("narrow", "wide"),
        P(("groups", "wide"), "narrow", None),
        P(("groups", "wide"), None, "narrow"),
        P(("groups", "wide"), None),
        P("groups"),
    )
    out_specs = (
        P(("groups", "wide"), "narrow"),
        P(("groups", "wide"), "narrow", None),
        P(("groups", "wide"), None, "narrow"),
    )
    shape = mesh.shape
    small = (shape["groups"], shape["wide"], shape["narrow"]) == (2, 8, 2)
    body = fused_body if small else plain_body
    return jax.shard_map(body, mesh=mesh, in_specs=in_specs, out_specs=out_specs, check_vma=False)
```
